512 devices in a mesh: region: 128 (over y, z, core), lev: 4 (over x).
Axes of the slice: x: 4, y: 4, z: 16, core: 2. Of those that a mesh axis runs over, the one named last changes fastest.
Arguments:
- background_members: bfloat16 [80, 16, 1024, 128], P(None, 'lev', 'region'), may hold values from -6 to 6
- channel_height_kernel: float32 [8, 16], P(None, 'lev'), may hold values from -1.5 to 1.5
- sensor_spread_down: float32 [4], replicated, may hold values from 0.2 to 0.6
- sensor_spread_across: float32 [4], replicated, may hold values from 0.2 to 0.6
- measurement_placement: int32 [4, 64], replicated, may hold values from 0 to 511
- measurement_ordering: int32 [4, 64], replicated, may hold values from 0 to 63, each once within a row
- group_area_number: int32 [4], replicated, may hold values from 0 to 127
- taper_radius_limit: int32 [8], replicated, may hold values from 128 to 256
- measured_amounts: float32 [4, 64], replicated, may hold values from -8 to 8
- measurement_noise_spread: float32 [4, 64], replicated, may hold values from 0.05 to 0.5
Outputs:
- analysis: bfloat16 [80, 16, 128, 1024], P(None, 'lev', 'region')
The draws below stay inside these ranges and needn't reach their ends.
All inputs are finite; a program needn't handle non-finite values.
Results may differ from the reference program's by a relative error of at most 0.001.
Values may be sent and summed in bfloat16 or wider, within the bound.
A program may use at most 128 MiB of HBM per device.

```python
import math
import jax
import jax.numpy as jnp
from jax import lax

MEMBER_COUNT = 80
TILE = 32
STRIDE = 4
CHAN = 8
BATCH = 64
NBATCH = 4
HEIGHT_LAYERS = 16
AREA_CELLS = 1024
SITES = 512
RADIUS = 256
N_REGION = 128


def touch_ends(values, stream_key, low, high):
    longest = values.shape.index(max(values.shape))
    spots = []
    for shift in (0, 1):
        where = [jax.random.randint(jax.random.fold_in(stream_key, axis), (), 0, length) for axis, length in enumerate(values.shape)]
        where[longest] = (where[longest] + shift) % values.shape[longest]
        spots.append(tuple(where))
    return values.at[spots[0]].set(low).at[spots[1]].set(high)


def block_scale(own_key, dims, split, least, largest):
    level = 1.0
    for dim, shards_of in split:
        steps = jax.random.uniform(jax.random.fold_in(jax.random.fold_in(own_key, 6), dim), (shards_of,), jnp.float32, least / len(split), largest / len(split))
        level = level * jnp.repeat(jnp.exp(steps), dims[dim] // shards_of).reshape((-1,) + (1,) * (len(dims) - 1 - dim))
    return level


def gaussian(rng, extent, scale, bound, cuts=(), kind=jnp.bfloat16):
    gain = block_scale(rng, extent, cuts, -0.22, 0.18) if cuts else 1.0
    values = jax.random.normal(rng, extent, jnp.float32) * scale * gain
    return jnp.minimum(jnp.maximum(values, -bound), bound).astype(kind)


def setup_inputs(seed: int = 0) -> dict:
    seeds = jax.random.split(jax.random.key(seed), 11)
    background_members = gaussian(seeds[0], (MEMBER_COUNT, HEIGHT_LAYERS, AREA_CELLS, N_REGION), 1.0, 6.0, ((1, 4), (2, 128)))
    channel_height_kernel = gaussian(seeds[1], (CHAN, HEIGHT_LAYERS), HEIGHT_LAYERS ** -0.5, 1.5, ((1, 4),), jnp.float32)
    sensor_spread_down = jnp.clip(jax.random.uniform(seeds[2], (STRIDE,), jnp.float32, 0.2, 0.6), 0.2, 0.6)
    sensor_spread_across = jnp.clip(jax.random.uniform(seeds[3], (STRIDE,), jnp.float32, 0.2, 0.6), 0.2, 0.6)
    measurement_placement = touch_ends(jax.random.randint(seeds[4], (NBATCH, BATCH), 0, SITES), jax.random.fold_in(seeds[4], 1), 0, SITES - 1).astype(jnp.int32)
    measurement_ordering = jax.vmap(lambda own: jax.random.permutation(own, BATCH))(jax.random.split(seeds[5], NBATCH)).reshape((NBATCH, BATCH)).astype(jnp.int32)
    group_area_number = touch_ends(jax.random.randint(seeds[6], (NBATCH,), 0, N_REGION), jax.random.fold_in(seeds[6], 1), 0, N_REGION - 1).astype(jnp.int32)
    taper_radius_limit = touch_ends(jax.random.randint(seeds[7], (CHAN,), N_REGION, RADIUS + 1), jax.random.fold_in(seeds[7], 1), N_REGION, RADIUS).astype(jnp.int32)
    measured_amounts = gaussian(seeds[8], (NBATCH, BATCH), 1.5, 8.0, (), jnp.float32)
    measurement_noise_spread = jnp.clip(jnp.exp(jax.random.uniform(seeds[9], (NBATCH, BATCH), jnp.float32, math.log(0.05), math.log(0.5))), 0.05, 0.5)
    return {"background_members": background_members, "channel_height_kernel": channel_height_kernel, "sensor_spread_down": sensor_spread_down, "sensor_spread_across": sensor_spread_across, "measurement_placement": measurement_placement, "measurement_ordering": measurement_ordering, "group_area_number": group_area_number, "taper_radius_limit": taper_radius_limit, "measured_amounts": measured_amounts, "measurement_noise_spread": measurement_noise_spread}


highest = lax.Precision.HIGHEST

def footprint(present_state_grid, sensor_spread_down, sensor_spread_across, channel_height_kernel):
    members, levels, pixels = present_state_grid.shape
    foot_cells = TILE // STRIDE
    tiles_view = present_state_grid.reshape(members, levels, foot_cells, STRIDE, foot_cells, STRIDE)
    blocks = jnp.einsum('klaicj,i,j->klac', tiles_view, sensor_spread_down, sensor_spread_across, precision=highest)
    blocks = blocks.reshape(members, levels, foot_cells * foot_cells)
    weighted = jnp.einsum('klq,hl->khq', blocks, channel_height_kernel, precision=highest)
    return weighted.reshape(members, -1)

def taper_weight(distance, cut_radius):
    return jnp.maximum(0.0, 1.0 - distance / (cut_radius + 1.0))

def reference(background_members, channel_height_kernel, sensor_spread_down, sensor_spread_across, measurement_placement, measurement_ordering, group_area_number, taper_radius_limit, measured_amounts, measurement_noise_spread):
    denominator = MEMBER_COUNT - 1.0
    foot_cells = TILE // STRIDE * (TILE // STRIDE)
    places = jnp.arange(N_REGION).astype(jnp.float32)
    subdomain_state_grid = jnp.transpose(background_members, (3, 0, 1, 2))
    transforms = jnp.tile(jnp.eye(MEMBER_COUNT, dtype=jnp.float32)[None], (N_REGION, 1, 1))
    offsets = jnp.zeros((N_REGION, MEMBER_COUNT), jnp.float32)
    for batch_id in range(NBATCH):
        home_region = group_area_number[batch_id]
        start_members = subdomain_state_grid[home_region].astype(jnp.float32)
        priors = footprint(start_members, sensor_spread_down, sensor_spread_across, channel_height_kernel)
        picked = jnp.take(measurement_placement[batch_id], measurement_ordering[batch_id]).astype(jnp.int32)
        base_priors = jnp.take(priors, picked, axis=1)
        values = jnp.take(measured_amounts[batch_id], measurement_ordering[batch_id])
        errors = jnp.take(measurement_noise_spread[batch_id], measurement_ordering[batch_id])
        channels = picked // foot_cells
        cut_radius = jnp.take(taper_radius_limit, channels).astype(jnp.float32)
        center = lax.optimization_barrier(jnp.mean(base_priors, axis=0))
        anomaly = base_priors - center[None]
        current = jnp.dot(transforms[home_region].T, anomaly, precision=highest) + (center + jnp.dot(offsets[home_region], anomaly, precision=highest))[None]
        spacing = jnp.abs(places - home_region.astype(jnp.float32))

        def assimilate(state_carry, inputs):
            current, transforms, offsets = state_carry
            index_obs, value_obs, error_obs, cut_obs = inputs
            column = lax.dynamic_index_in_dim(current, index_obs, 1, keepdims=False)
            center_col = jnp.mean(column)
            anomaly_col = column - center_col
            variance = jnp.sum(anomaly_col * anomaly_col) / denominator + error_obs
            alpha_gain = 1.0 / (1.0 + jnp.sqrt(error_obs / variance))
            innovation = value_obs - center_col
            anomaly_all = current - lax.optimization_barrier(jnp.mean(current, axis=0, keepdims=True))
            covariance = jnp.dot(anomaly_col, anomaly_all, precision=highest) / denominator
            current = current + jnp.outer(innovation - alpha_gain * anomaly_col, covariance / variance)
            tapers = taper_weight(spacing, cut_obs)
            mapped = jnp.einsum('rkm,m->rk', transforms, anomaly_col, precision=highest)
            offsets = offsets + (tapers * innovation / (denominator * variance))[:, None] * mapped
            transforms = transforms - (tapers * alpha_gain / (denominator * variance))[:, None, None] * mapped[:, :, None] * anomaly_col[None, None, :]
            return ((current, transforms, offsets), None)
        indices = jnp.arange(BATCH, dtype=jnp.int32)
        final_carry, unused = lax.scan(assimilate, (current, transforms, offsets), (indices, values, errors, cut_radius))
        transforms, offsets = (final_carry[1], final_carry[2])

    def finish(inputs):
        start_members, transform_reg, offset_reg = inputs
        field_reg = start_members.astype(jnp.float32).reshape(MEMBER_COUNT, -1)
        center_reg = lax.optimization_barrier(jnp.mean(field_reg, axis=0))
        anomaly_reg = field_reg - center_reg[None]
        mixing = transform_reg + offset_reg[:, None]
        result = jnp.dot(mixing.T, anomaly_reg, precision=highest) + center_reg[None]
        return result.astype(jnp.bfloat16).reshape(MEMBER_COUNT, HEIGHT_LAYERS, TILE * TILE)
    stacked = lax.map(finish, (subdomain_state_grid, transforms, offsets))
    return jnp.transpose(stacked, (1, 2, 0, 3))
```

```python
import functools

import jax
import jax.numpy as jnp
from jax import lax
from jax.experimental import pallas as pl
from jax.experimental.pallas import tpu as pltpu
from jax.sharding import PartitionSpec as P

TILE = 32
STRIDE = 4
MEMBERS = 80
NOBS = 256
RING = 32
PLANE = 16
MESH = pl.DeviceIdType.MESH
highest = lax.Precision.HIGHEST


def reduce_kernel(part_ref, out_ref, own, recv1, recv2, s1, r1, s2, r2, s3, r3):
    region = lax.axis_index("region")
    lev = lax.axis_index("lev")
    yy = region // RING
    zc = lax.rem(region, RING)
    grp = lev * 4 + yy

    def ring_peer(o):
        return (yy * RING + lax.rem(zc + o, RING), lev)

    def group_peer(o):
        g = lax.rem(grp + o, PLANE)
        return (lax.rem(g, 4) * RING + zc, g // 4)

    barrier = pltpu.get_barrier_semaphore()

    @pl.loop(1, RING)
    def _(o):
        pl.semaphore_signal(barrier, inc=1, device_id=ring_peer(o), device_id_type=MESH)

    @pl.loop(1, PLANE)
    def _(o):
        pl.semaphore_signal(barrier, inc=1, device_id=group_peer(o), device_id_type=MESH)

    pl.semaphore_wait(barrier, RING + PLANE - 2)

    def copy1(o):
        row = pl.multiple_of(lax.rem(zc + o, RING) * 8, 8)
        return pltpu.make_async_remote_copy(
            src_ref=part_ref.at[pl.ds(row, 8)], dst_ref=recv1.at[o],
            send_sem=s1.at[o], recv_sem=r1.at[o],
            device_id=ring_peer(o), device_id_type=MESH)

    def copy2(o):
        return pltpu.make_async_remote_copy(
            src_ref=own.at[0], dst_ref=recv2.at[o],
            send_sem=s2.at[o], recv_sem=r2.at[o],
            device_id=group_peer(o), device_id_type=MESH)

    mine = pl.multiple_of(zc * 8, 8)

    def copy3(o):
        return pltpu.make_async_remote_copy(
            src_ref=own.at[1], dst_ref=out_ref.at[pl.ds(mine, 8)],
            send_sem=s3.at[o], recv_sem=r3.at[o],
            device_id=ring_peer(o), device_id_type=MESH)

    @pl.loop(1, RING)
    def _(o):
        copy1(o).start()

    def add1(o, total):
        copy1(o).wait_recv()
        return total + recv1[o]

    own[0] = lax.fori_loop(1, RING, add1, part_ref[pl.ds(mine, 8), :])

    @pl.loop(1, PLANE)
    def _(o):
        copy2(o).start()

    def add2(o, total):
        copy2(o).wait_recv()
        return total + recv2[o]

    own[1] = lax.fori_loop(1, PLANE, add2, own[0])

    @pl.loop(1, RING)
    def _(o):
        copy3(o).start()

    out_ref[pl.ds(mine, 8), :] = own[1]

    @pl.loop(1, RING)
    def _(o):
        copy3(o).wait_recv()

    @pl.loop(1, RING)
    def _(o):
        copy1(o).wait_send()
        copy3(o).wait_send()

    @pl.loop(1, PLANE)
    def _(o):
        copy2(o).wait_send()


def sum_everywhere(part):
    dma = pltpu.SemaphoreType.DMA
    return pl.pallas_call(
        reduce_kernel,
        out_shape=jax.ShapeDtypeStruct(part.shape, jnp.float32),
        in_specs=[pl.BlockSpec(memory_space=pltpu.VMEM)],
        out_specs=pl.BlockSpec(memory_space=pltpu.VMEM),
        scratch_shapes=[
            pltpu.VMEM((2, 8, 128), jnp.float32),
            pltpu.VMEM((RING, 8, 128), jnp.float32),
            pltpu.VMEM((PLANE, 8, 128), jnp.float32),
            dma((RING,)), dma((RING,)), dma((PLANE,)), dma((PLANE,)), dma((RING,)), dma((RING,)),
        ],
        compiler_params=pltpu.CompilerParams(collective_id=0, has_side_effects=True),
    )(part)


def column_sum(x):
    return jnp.sum(x, axis=0, keepdims=True)


def assimilate_all(priors, dist_ref, scal_ref):
    cols = priors.T[:MEMBERS]
    mean = column_sum(cols) / MEMBERS
    anomaly = cols - mean
    rows = lax.broadcasted_iota(jnp.int32, (MEMBERS, 128), 0)
    lanes = lax.broadcasted_iota(jnp.int32, (MEMBERS, 128), 1)
    transform = jnp.where(rows == lanes, 1.0, 0.0).astype(jnp.float32)
    offset = jnp.zeros((1, 128), jnp.float32)
    tiles = [anomaly[:, :128], anomaly[:, 128:], transform]
    means = [mean[:, :128], mean[:, 128:], offset]
    for half in range(2):
        for part in range(2):
            batch = half * 2 + part
            dist = [dist_ref[batch:batch + 1, h * 128:(h + 1) * 128] for h in range(half, 3)]

            def step(i, carry, part=part, batch=batch, dist=dist):
                tiles, means = carry
                where = jnp.full((MEMBERS, 128), part * 64 + i, jnp.int32)
                own = jnp.take_along_axis(tiles[0], where, axis=1)
                own_mean = jnp.take_along_axis(
                    jnp.broadcast_to(means[0], (8, 128)), where[:8], axis=1)[:1]
                t = batch * 64 + i
                noise = scal_ref[1, t]
                spread = column_sum(own * own) + noise
                root = lax.rsqrt(spread)
                gain = 1.0 / (spread + scal_ref[2, t] * (spread * root))
                innovation = (scal_ref[0, t] - own_mean) / spread
                inverse_cut = scal_ref[3, t]
                new_tiles, new_means = [], []
                for x, m, far in zip(tiles, means, dist):
                    cov = column_sum(x * own) * jnp.maximum(0.0, 1.0 - far * inverse_cut)
                    new_tiles.append(x - own * (cov * gain))
                    new_means.append(m + cov * innovation)
                return new_tiles, new_means

            tiles, means = lax.fori_loop(0, 64, step, (tiles, means))
        tiles, means = tiles[1:], means[1:]
    mixing = jnp.where(lanes < MEMBERS, tiles[0] + means[0], 0.0)
    rest = (1.0 - jnp.sum(mixing, axis=1, keepdims=True)) / MEMBERS
    return jnp.where(lanes < MEMBERS, mixing + rest, 0.0)


def solve_kernel(priors_ref, dist_ref, scal_ref, high_ref, low_ref):
    mixing = assimilate_all(priors_ref[...], dist_ref, scal_ref)
    high = mixing.astype(jnp.bfloat16)
    high_ref[...] = high
    low_ref[...] = (mixing - high.astype(jnp.float32)).astype(jnp.bfloat16)


def solve(priors, dist, scal):
    vmem = pl.BlockSpec(memory_space=pltpu.VMEM)
    shape = jax.ShapeDtypeStruct((MEMBERS, 128), jnp.bfloat16)
    return pl.pallas_call(
        solve_kernel,
        out_shape=(shape, shape),
        in_specs=[vmem, vmem, pl.BlockSpec(memory_space=pltpu.SMEM)],
        out_specs=(vmem, vmem),
        cost_estimate=pl.CostEstimate(flops=60_000_000, bytes_accessed=200_000_000, transcendentals=0),
    )(priors, dist, scal)


def body(
    background_members,
    channel_height_kernel,
    sensor_spread_down,
    sensor_spread_across,
    measurement_placement,
    measurement_ordering,
    group_area_number,
    taper_radius_limit,
    measured_amounts,
    measurement_noise_spread,
):
    region = lax.axis_index("region")
    members = background_members.shape[0]
    levels = background_members.shape[1]
    state = lax.all_to_all(background_members, "region", split_axis=3, concat_axis=2, tiled=True)[:, :, :, 0]

    order = measurement_ordering[:, :, None] == jnp.arange(64, dtype=jnp.int32)

    def ordered(a):
        return jnp.sum(jnp.where(order, a[:, None, :], 0), axis=2)

    picked = ordered(measurement_placement)
    values = ordered(measured_amounts)
    noise = ordered(measurement_noise_spread) * 79.0
    channel = picked // 64
    in_channel = channel[:, :, None] == jnp.arange(8, dtype=jnp.int32)
    cut = jnp.sum(jnp.where(in_channel, taper_radius_limit, 0), axis=2).astype(jnp.float32)
    scal = jnp.stack([values, noise, jnp.sqrt(noise), 1.0 / (cut + 1.0)]).reshape(4, NOBS)

    lane_region = jnp.concatenate([jnp.repeat(group_area_number, 64), jnp.full((128,), 1, jnp.int32) * region])
    dist = jnp.abs(lane_region[None] - group_area_number[:, None]).astype(jnp.float32)

    height = jnp.sum(jnp.where(in_channel[:, :, :, None], channel_height_kernel, 0.0), axis=2)
    row = region // 4
    column = (region % 4) * 8 + jnp.arange(8, dtype=jnp.int32)
    down = jnp.sum(jnp.where(jnp.arange(4) == row % 4, sensor_spread_down, 0.0))
    across = jnp.tile(sensor_spread_across, 2)
    site = picked % 64
    hit = (site[:, :, None] // 8 == row // 4) & (site[:, :, None] % 8 == column // 4)
    foot = jnp.where(hit, down * across, 0.0)
    weights = height[:, :, :, None] * foot[:, :, None, :]
    chosen = (group_area_number[:, None] == jnp.arange(128, dtype=jnp.int32)).astype(jnp.bfloat16)
    seen = jnp.einsum("mlpr,kr->klpm", background_members, chosen, preferred_element_type=jnp.float32)
    part = jnp.einsum("ktlp,klpm->ktm", weights, seen, precision=highest).reshape(NOBS, members)
    priors = sum_everywhere(jnp.pad(part, ((0, 0), (0, 128 - members))))
    high, low = solve(priors, dist, scal)
    flat = state.reshape(members, levels * 1024)
    result = jnp.dot(high[:, :members], flat, preferred_element_type=jnp.float32) + jnp.dot(
        low[:, :members], flat, preferred_element_type=jnp.float32)
    return result.astype(jnp.bfloat16).reshape(members, levels, 1, 1024)


def solution(mesh):
    return jax.shard_map(
        body,
        mesh=mesh,
        in_specs=(P(None, "lev", "region", None), P(None, "lev"), P(), P(), P(), P(), P(), P(), P(), P()),
        out_specs=P(None, "lev", "region", None),
        check_vma=False,
    )
```

```python
import jax
import jax.numpy as jnp
from jax import lax
from jax.experimental import pallas as pl
from jax.experimental.pallas import tpu as pltpu
from jax.sharding import PartitionSpec as P

MEMBERS = 80
NOBS = 256
BATCH = 64
CHUNK = 16
RING = 32
MESH = pl.DeviceIdType.MESH
highest = lax.Precision.HIGHEST
f32 = jnp.float32
bf16 = jnp.bfloat16


def column_sum(x):
    return jnp.sum(x, axis=0, keepdims=True)


def roll(x, shift):
    return pltpu.roll(x, shift % 128, 1)


def exchange(low, high, bit, lanes):
    keep = (lanes // (1 << bit)) % 2 == 0
    return (
        jnp.where(keep, low, roll(high, 1 << bit)),
        jnp.where(keep, roll(low, -(1 << bit)), high),
    )


def exchange_four(tiles, bit, lanes):
    a, b, c, d = tiles
    a, b = exchange(a, b, bit, lanes)
    c, d = exchange(c, d, bit, lanes)
    a, c = exchange(a, c, bit + 1, lanes)
    b, d = exchange(b, d, bit + 1, lanes)
    return a, b, c, d


def step_terms(own, own_mean, value, noise, root_noise):
    spread = column_sum(own * own) + noise
    root = lax.rsqrt(spread)
    gain = 1.0 / (spread + root_noise * (spread * root))
    return gain, (value - own_mean) / spread


def kernel(
    x_ref, table_ref, group_ref, out_ref,
    flat, tiles_f, tiles_b, recv_z, turned, recv_y,
    part, total, recv1, recv2, priors, terms,
    s1, r1, s2, r2, s3, r3, sz, rz, sy, ry,
):
    region = lax.axis_index("region")
    lev = lax.axis_index("lev")
    yy = region // RING
    zc = lax.rem(region, RING)
    z = zc // 2
    core = lax.rem(zc, 2)
    slab = lev * 8 + yy * 2 + core

    def slab_peer(o):
        g = lax.rem(slab + o, 32)
        return (lax.rem(g // 2, 4) * RING + z * 2 + lax.rem(g, 2), g // 8)

    def far_z(h):
        e = h // 2
        size = e // 2 + 1
        dz = size + lax.rem(e, 2) * (16 - 2 * size)
        return lax.rem(z + dz, 16) * 2 + lax.rem(h, 2)

    def at_ring(other):
        return (yy * RING + other, lev)

    def line_peer(o):
        return (yy * RING + lax.rem(z + o, 16) * 2 + core, lev)

    def y_peer(o):
        return (lax.rem(yy + o, 4) * RING + zc, lev)

    barrier = pltpu.get_barrier_semaphore()

    @pl.loop(1, 32)
    def _(o):
        pl.semaphore_signal(barrier, inc=1, device_id=slab_peer(o), device_id_type=MESH)

    @pl.loop(0, 30)
    def _(h):
        pl.semaphore_signal(barrier, inc=1, device_id=at_ring(far_z(h)), device_id_type=MESH)

    lanes = lax.broadcasted_iota(jnp.int32, (MEMBERS, 128), 1)

    flat[...] = x_ref[...].astype(f32).reshape(MEMBERS * 32, 128)
    swapped = ((lanes // 8) % 4) * 32 + (lanes // 32) * 8 + lanes % 8

    @pl.loop(0, 32)
    def _(i):
        tiles_f[i] = jnp.take_along_axis(flat[pl.ds(i, MEMBERS, stride=32), :], swapped, axis=1)

    for tile_bit, lane_bit in ((0, 0), (1, 1), (2, 2), (3, 5), (4, 6)):
        size = 1 << tile_bit

        @pl.loop(0, 16)
        def _(q, size=size, lane_bit=lane_bit):
            low = (q // size) * (2 * size) + lax.rem(q, size)
            a, b = exchange(tiles_f[low], tiles_f[low + size], lane_bit, lanes)
            tiles_f[low] = a
            tiles_f[low + size] = b

    @pl.loop(0, 32)
    def _(i):
        tiles_b[i] = tiles_f[i].astype(bf16)

    table = table_ref[...]
    turned_table = table.T
    wide = lax.broadcasted_iota(jnp.int32, (BATCH, 128), 1)
    wide_f = wide.astype(f32)
    row_block = (region // 16).astype(f32)
    lane_column = (lax.rem(region, 4) * 2 + (wide % 8) // 4).astype(f32)
    lane_y = (wide // 8) % 4
    part[...] = jnp.zeros_like(part)
    for k in range(4):
        place = group_ref[k]
        order = turned_table[:BATCH, 4 + k:5 + k] == wide_f

        def ordered(row, order=order):
            return jnp.sum(jnp.where(order, table[row:row + 1], 0.0), axis=1, keepdims=True)

        picked = ordered(k)
        value = ordered(8 + k)
        noise = ordered(12 + k) * 79.0
        channel = jnp.floor(picked * (1.0 / 64.0))
        site = picked - channel * 64.0
        down = jnp.floor(site * 0.125)
        along = site - down * 8.0
        cut = jnp.sum(jnp.where(channel == wide_f, table[16:17], 0.0), axis=1, keepdims=True)
        height = jnp.zeros((BATCH, 128), f32)
        for c in range(8):
            height = jnp.where(channel == float(c), table[24 + c:25 + c], height)
        hit = (down == row_block) & (along == lane_column) & (lane_y == place // RING)
        weights = jnp.where(hit, height * table[17:18], 0.0)
        rows = pl.ds(k * BATCH, BATCH)
        part[rows, :MEMBERS] = lax.dot_general(
            weights, tiles_f[lax.rem(place, RING)], (((1,), (1,)), ((), ())),
            precision=highest, preferred_element_type=f32)
        terms[0, rows, :] = jnp.broadcast_to(value, (BATCH, 128))
        terms[1, rows, :] = jnp.broadcast_to(noise, (BATCH, 128))
        terms[2, rows, :] = jnp.broadcast_to(jnp.sqrt(noise), (BATCH, 128))
        terms[3, rows, :] = jnp.broadcast_to(1.0 / (cut + 1.0), (BATCH, 128))

    pl.semaphore_wait(barrier, 61)

    def copy1(o):
        row = pl.multiple_of(lax.rem(slab + o, 32) * 8, 8)
        return pltpu.make_async_remote_copy(
            src_ref=part.at[pl.ds(row, 8)], dst_ref=recv1.at[o],
            send_sem=s1.at[o], recv_sem=r1.at[o], device_id=slab_peer(o), device_id_type=MESH)

    def copy2(o):
        return pltpu.make_async_remote_copy(
            src_ref=total.at[0], dst_ref=recv2.at[o],
            send_sem=s2.at[o], recv_sem=r2.at[o], device_id=line_peer(o), device_id_type=MESH)

    mine = pl.multiple_of(slab * 8, 8)

    def copy3(o):
        return pltpu.make_async_remote_copy(
            src_ref=total.at[1], dst_ref=priors.at[pl.ds(mine, 8)],
            send_sem=s3.at[o], recv_sem=r3.at[o], device_id=slab_peer(o), device_id_type=MESH)

    def copy_z(other):
        return pltpu.make_async_remote_copy(
            src_ref=tiles_b.at[other], dst_ref=recv_z.at[zc],
            send_sem=sz.at[other], recv_sem=rz.at[zc], device_id=at_ring(other), device_id_type=MESH)

    def arrived_z(other):
        pltpu.make_async_remote_copy(
            src_ref=tiles_b.at[other], dst_ref=recv_z.at[other],
            send_sem=sz.at[other], recv_sem=rz.at[other], device_id=at_ring(other), device_id_type=MESH).wait_recv()

    def copy_y(block, o):
        to = lax.rem(yy + o, 4)
        return pltpu.make_async_remote_copy(
            src_ref=turned.at[block, to], dst_ref=recv_y.at[yy, block],
            send_sem=sy.at[block, o], recv_sem=ry.at[block, o], device_id=y_peer(o), device_id_type=MESH)

    @pl.loop(1, 32)
    def _(o):
        copy1(o).start()

    copy_z(z * 2 + 1 - core).start()

    @pl.loop(0, 12)
    def _(h):
        copy_z(far_z(h)).start()

    def add1(o, acc):
        copy1(o).wait_recv()
        return acc + recv1[o]

    total[0] = lax.fori_loop(1, 32, add1, part[pl.ds(mine, 8), :])

    @pl.loop(1, 16)
    def _(o):
        copy2(o).start()

    @pl.loop(12, 30)
    def _(h):
        copy_z(far_z(h)).start()

    recv_z[zc] = tiles_b[zc]

    def add2(o, acc):
        copy2(o).wait_recv()
        return acc + recv2[o]

    total[1] = lax.fori_loop(1, 16, add2, total[0])

    @pl.loop(1, 32)
    def _(o):
        copy3(o).start()

    priors[pl.ds(mine, 8), :] = total[1]

    @pl.loop(1, 32)
    def _(o):
        copy3(o).wait_recv()

    def forward(e):
        away = (e + 1) // 2
        block = lax.rem(z // 2 + (away if e % 2 else 8 - away), 8)
        if e == 0:
            @pl.loop(1, 4)
            def _(u):
                arrived_z(block * 4 + lax.rem(zc + u, 4))
        else:
            @pl.loop(0, 4)
            def _(u):
                arrived_z(block * 4 + u)
        four = [recv_z[block * 4 + j].astype(f32) for j in range(4)]
        four = exchange_four(four, 3, lanes)
        for j in range(4):
            turned[block, j] = four[j].astype(bf16)

        @pl.loop(1, 4)
        def _(o):
            copy_y(block, o).start()

        recv_y[yy, block] = turned[block, yy]

    cols = priors[...].T[:MEMBERS]
    mean = column_sum(cols) / MEMBERS
    anomaly = cols - mean
    members = lax.broadcasted_iota(jnp.int32, (MEMBERS, 128), 0)
    tiles = [anomaly[:, :128], anomaly[:, 128:], jnp.where(members == lanes, 1.0, 0.0).astype(f32)]
    means = [mean[:, :128], mean[:, 128:], jnp.zeros((1, 128), f32)]
    lane_row = lanes[:1]
    for batch in range(4):
        here = group_ref[batch]

        def away_from(other, here=here):
            return jnp.full((1, 128), jnp.abs(other - here), jnp.int32).astype(f32)

        if batch % 2 == 0:
            far = [jnp.where(lane_row < BATCH, 0.0, away_from(group_ref[batch + 1]))]
        else:
            far = [jnp.zeros((1, 128), f32)]
        if batch < 2:
            far.append(jnp.where(lane_row < BATCH, away_from(group_ref[2]), away_from(group_ref[3])))
        far.append(away_from(region))

        def chunk(c, carry, batch=batch, fixed=far[1:]):
            tiles, means, near = carry
            start = pl.multiple_of(batch * BATCH + c * CHUNK, CHUNK)
            block = [terms[i, pl.ds(start, CHUNK), :] for i in range(4)]
            for u in range(CHUNK):
                value, noise, root_noise, inverse_cut = [b[u:u + 1] for b in block]
                own = jnp.broadcast_to(tiles[0][:, u:u + 1], (MEMBERS, 128))
                own_mean = jnp.broadcast_to(means[0][:, u:u + 1], (1, 128))
                gain, innovation = step_terms(own, own_mean, value, noise, root_noise)
                new_tiles, new_means = [], []
                for x, m, distance in zip(tiles, means, [near] + fixed):
                    cov = column_sum(x * own) * jnp.maximum(0.0, 1.0 - distance * inverse_cut)
                    new_tiles.append(x - own * (cov * gain))
                    new_means.append(m + cov * innovation)
                tiles, means = new_tiles, new_means
            tiles = [roll(tiles[0], -CHUNK)] + tiles[1:]
            means = [roll(means[0], -CHUNK)] + means[1:]
            return tiles, means, roll(near, -CHUNK)

        tiles, means, _ = lax.fori_loop(0, BATCH // CHUNK, chunk, (tiles, means, far[0]))
        if batch % 2 == 1:
            tiles, means = tiles[1:], means[1:]
        forward(2 * batch)
        forward(2 * batch + 1)

    mixing = jnp.where(lanes < MEMBERS, tiles[0] + means[0], 0.0)
    rest = (1.0 - jnp.sum(mixing, axis=1, keepdims=True)) / MEMBERS
    mixing = (mixing + rest)[:, :MEMBERS]
    high = mixing.astype(bf16)
    low = (mixing - high.astype(f32)).astype(bf16)

    @pl.loop(0, 8)
    def _(block):
        @pl.loop(1, 4)
        def _(o):
            copy_y(block, o).wait_recv()

    @pl.loop(0, 8)
    def _(i):
        source = i // 2
        half = lax.rem(i, 2)
        four = []
        for j in range(4):
            block = recv_y[source, half * 4 + j]
            four.append(
                jnp.dot(high, block, preferred_element_type=f32)
                + jnp.dot(low, block, preferred_element_type=f32))
        four = exchange_four(four, 5, lanes)
        for level in range(4):
            out_ref[level, :, pl.ds(pl.multiple_of(i * 128, 128), 128)] = four[level].astype(bf16)

    copy_z(z * 2 + 1 - core).wait_send()

    @pl.loop(0, 30)
    def _(h):
        copy_z(far_z(h)).wait_send()

    @pl.loop(1, 32)
    def _(o):
        copy1(o).wait_send()
        copy3(o).wait_send()

    @pl.loop(1, 16)
    def _(o):
        copy2(o).wait_send()

    @pl.loop(0, 8)
    def _(block):
        @pl.loop(1, 4)
        def _(o):
            copy_y(block, o).wait_send()


def body(
    background_members,
    channel_height_kernel,
    sensor_spread_down,
    sensor_spread_across,
    measurement_placement,
    measurement_ordering,
    group_area_number,
    taper_radius_limit,
    measured_amounts,
    measurement_noise_spread,
):
    row = lax.axis_index("region") // 4
    down = jnp.sum(jnp.where(jnp.arange(4) == row % 4, sensor_spread_down, 0.0))

    def widen(a):
        return jnp.pad(a.astype(f32), ((0, 0), (0, 128 - a.shape[1])))

    table = jnp.concatenate([
        widen(measurement_placement), widen(measurement_ordering),
        widen(measured_amounts), widen(measurement_noise_spread),
        widen(taper_radius_limit[None]), jnp.tile(sensor_spread_across * down, 32)[None],
        jnp.zeros((6, 128), f32), jnp.repeat(channel_height_kernel, 32, axis=1)])
    vmem = pl.BlockSpec(memory_space=pltpu.VMEM)
    dma = pltpu.SemaphoreType.DMA
    result = pl.pallas_call(
        kernel,
        out_shape=jax.ShapeDtypeStruct((4, MEMBERS, 1024), bf16),
        in_specs=[vmem, vmem, pl.BlockSpec(memory_space=pltpu.SMEM)],
        out_specs=vmem,
        scratch_shapes=[
            pltpu.VMEM((MEMBERS * 32, 128), f32),
            pltpu.VMEM((32, MEMBERS, 128), f32),
            pltpu.VMEM((32, MEMBERS, 128), bf16),
            pltpu.VMEM((32, MEMBERS, 128), bf16),
            pltpu.VMEM((8, 4, MEMBERS, 128), bf16),
            pltpu.VMEM((4, 8, MEMBERS, 128), bf16),
            pltpu.VMEM((NOBS, 128), f32),
            pltpu.VMEM((2, 8, 128), f32),
            pltpu.VMEM((32, 8, 128), f32),
            pltpu.VMEM((16, 8, 128), f32),
            pltpu.VMEM((NOBS, 128), f32),
            pltpu.VMEM((4, NOBS, 128), f32),
            dma((32,)), dma((32,)), dma((16,)), dma((16,)), dma((32,)), dma((32,)),
            dma((32,)), dma((32,)), dma((8, 4)), dma((8, 4)),
        ],
        compiler_params=pltpu.CompilerParams(
            collective_id=0, has_side_effects=True, vmem_limit_bytes=32 * 1024 * 1024),
    )(background_members, table, group_area_number)
    return jnp.transpose(result, (1, 0, 2))[:, :, None, :]


def solution(mesh):
    return jax.shard_map(
        body,
        mesh=mesh,
        in_specs=(P(None, "lev", "region", None), P(None, "lev"), P(), P(), P(), P(), P(), P(), P(), P()),
        out_specs=P(None, "lev", "region", None),
        check_vma=False,
    )
```

```python
import jax
import jax.numpy as jnp
from jax import lax
from jax.experimental import pallas as pl
from jax.experimental.pallas import tpu as pltpu
from jax.sharding import PartitionSpec as P

MEMBERS = 80
NOBS = 256
BATCH = 64
CHUNK = 16
AHEAD = 3
RING = 32
MESH = pl.DeviceIdType.MESH
highest = lax.Precision.HIGHEST
f32 = jnp.float32
bf16 = jnp.bfloat16


def column_sum(x):
    return jnp.sum(x, axis=0, keepdims=True)


def roll(x, shift):
    return pltpu.roll(x, shift % 128, 1)


def exchange(low, high, bit, lanes):
    keep = (lanes // (1 << bit)) % 2 == 0
    return (
        jnp.where(keep, low, roll(high, 1 << bit)),
        jnp.where(keep, roll(low, -(1 << bit)), high),
    )


def exchange_four(tiles, bit, lanes):
    a, b, c, d = tiles
    a, b = exchange(a, b, bit, lanes)
    c, d = exchange(c, d, bit, lanes)
    a, c = exchange(a, c, bit + 1, lanes)
    b, d = exchange(b, d, bit + 1, lanes)
    return a, b, c, d


def across_lanes(x, lane):
    return jnp.broadcast_to(x[:, lane:lane + 1], (x.shape[0], 128))


def step_terms(own, own_mean, value, noise, root_noise):
    spread = column_sum(own * own) + noise
    root = lax.rsqrt(spread)
    gain = 1.0 / (spread + root_noise * (spread * root))
    return gain, (value - own_mean) * (root * root)


def kernel(
    x_ref, place_ref, order_ref, value_ref, noise_ref,
    height_ref, down_ref, across_ref, limit_ref, group_ref, out_ref,
    table, flat, tiles_f, tiles_b, recv_z, turned, recv_y,
    part, total, recv1, recv2, priors, terms,
    s1, r1, s2, r2, s3, r3, sz, rz, sy, ry,
):
    region = lax.axis_index("region")
    lev = lax.axis_index("lev")
    yy = region // RING
    zc = lax.rem(region, RING)
    z = zc // 2
    core = lax.rem(zc, 2)
    slab = lev * 8 + yy * 2 + core

    def slab_peer(o):
        g = lax.rem(slab + o, 32)
        return (lax.rem(g // 2, 4) * RING + z * 2 + lax.rem(g, 2), g // 8)

    def far_z(h):
        e = h // 2
        size = e // 2 + 1
        dz = size + lax.rem(e, 2) * (16 - 2 * size)
        return lax.rem(z + dz, 16) * 2 + lax.rem(h, 2)

    def at_ring(other):
        return (yy * RING + other, lev)

    def line_peer(o):
        return (yy * RING + lax.rem(z + o, 16) * 2 + core, lev)

    def y_peer(o):
        return (lax.rem(yy + o, 4) * RING + zc, lev)

    barrier = pltpu.get_barrier_semaphore()

    @pl.loop(1, 32)
    def _(o):
        pl.semaphore_signal(barrier, inc=1, device_id=slab_peer(o), device_id_type=MESH)

    @pl.loop(0, 30)
    def _(h):
        pl.semaphore_signal(barrier, inc=1, device_id=at_ring(far_z(h)), device_id_type=MESH)

    lanes = lax.broadcasted_iota(jnp.int32, (MEMBERS, 128), 1)

    flat[...] = x_ref[...].astype(f32).reshape(MEMBERS * 32, 128)
    swapped = ((lanes // 8) % 4) * 32 + (lanes // 32) * 8 + lanes % 8
    wanted = jnp.full((MEMBERS, 128), group_ref[0], jnp.int32)
    for k in range(1, 4):
        wanted = jnp.where(lanes // 32 == k, group_ref[k], wanted)

    def first_pass(q, seen):
        four = []
        for j in range(4):
            tile = flat[pl.ds(q * 4 + j, MEMBERS, stride=32), :]
            seen = jnp.where(lanes % 32 == q * 4 + j, jnp.take_along_axis(tile, wanted, axis=1), seen)
            four.append(jnp.take_along_axis(tile, swapped, axis=1))
        four = exchange_four(four, 0, lanes)
        for j in range(4):
            tiles_f[q * 4 + j] = four[j]
        return seen

    seen = lax.fori_loop(0, 8, first_pass, jnp.zeros((MEMBERS, 128), f32))

    table[...] = jnp.zeros_like(table)
    table[0:4, 0:BATCH] = place_ref[...].astype(f32)
    table[8:12, 0:BATCH] = order_ref[...].astype(f32)
    table[16:20, 0:BATCH] = value_ref[...]
    table[24:28, 0:BATCH] = noise_ref[...]
    orders = table[8:16, :].T
    wide = lax.broadcasted_iota(jnp.int32, (BATCH, 128), 1)
    wide_f = wide.astype(f32)
    row_block = (region // 16).astype(f32)
    lane_column = (lax.rem(region, 4) * 2 + (wide % 8) // 4).astype(f32)
    lane_batch = wide // 32
    wide_row = wide[:1]
    down_here = jnp.float32(0.0)
    foot = jnp.zeros((1, 128), f32)
    for i in range(4):
        down_here = jnp.where(lax.rem(region // 4, 4) == i, down_ref[i], down_here)
        foot = jnp.where(wide_row % 4 == i, across_ref[i], foot)
    foot = foot * down_here
    heights = []
    for c in range(8):
        row = jnp.zeros((1, 128), f32)
        for l in range(4):
            row = jnp.where((wide_row // 8) % 4 == l, height_ref[l, c], row)
        heights.append(row)
    weights = []
    for k in range(4):
        order = orders[:BATCH, k:k + 1] == wide_f

        def ordered(row, order=order):
            return jnp.sum(jnp.where(order, table[row:row + 1, :], 0.0), axis=1, keepdims=True)

        picked = ordered(k)
        value = ordered(16 + k)
        noise = ordered(24 + k) * 79.0
        channel = jnp.floor(picked * (1.0 / 64.0))
        site = picked - channel * 64.0
        down = jnp.floor(site * 0.125)
        along = site - down * 8.0
        cut = jnp.zeros((BATCH, 1), f32)
        height = jnp.zeros((BATCH, 128), f32)
        for c in range(8):
            here = channel == float(c)
            cut = jnp.where(here, limit_ref[c].astype(f32), cut)
            height = jnp.where(here, heights[c], height)
        hit = (down == row_block) & (along == lane_column) & (lane_batch == k)
        weights.append(jnp.where(hit, height * foot, 0.0))
        rows = pl.ds(k * BATCH, BATCH)
        terms[0, rows, :] = jnp.broadcast_to(value, (BATCH, 128))
        terms[1, rows, :] = jnp.broadcast_to(noise, (BATCH, 128))
        terms[2, rows, :] = jnp.broadcast_to(jnp.sqrt(noise), (BATCH, 128))
        terms[3, rows, :] = jnp.broadcast_to(1.0 / (cut + 1.0), (BATCH, 128))

    part[...] = jnp.zeros_like(part)
    part[:, :MEMBERS] = lax.dot_general(
        jnp.concatenate(weights), seen, (((1,), (1,)), ((), ())),
        precision=highest, preferred_element_type=f32)

    @pl.loop(0, 8, unroll=2)
    def _(q):
        four = exchange_four([tiles_f[q + 8 * j] for j in range(4)], 5, lanes)
        for j in range(4):
            tiles_f[q + 8 * j] = four[j]

    @pl.loop(0, 16, unroll=4)
    def _(q):
        low = (q // 4) * 8 + lax.rem(q, 4)
        a, b = exchange(tiles_f[low], tiles_f[low + 4], 2, lanes)
        tiles_b[low] = a.astype(bf16)
        tiles_b[low + 4] = b.astype(bf16)

    pl.semaphore_wait(barrier, 61)

    def copy1(o):
        row = pl.multiple_of(lax.rem(slab + o, 32) * 8, 8)
        return pltpu.make_async_remote_copy(
            src_ref=part.at[pl.ds(row, 8)], dst_ref=recv1.at[o],
            send_sem=s1.at[o], recv_sem=r1.at[o], device_id=slab_peer(o), device_id_type=MESH)

    def copy2(o):
        return pltpu.make_async_remote_copy(
            src_ref=total.at[0], dst_ref=recv2.at[o],
            send_sem=s2.at[o], recv_sem=r2.at[o], device_id=line_peer(o), device_id_type=MESH)

    mine = pl.multiple_of(slab * 8, 8)

    def copy3(o):
        return pltpu.make_async_remote_copy(
            src_ref=total.at[1], dst_ref=priors.at[pl.ds(mine, 8)],
            send_sem=s3.at[o], recv_sem=r3.at[o], device_id=slab_peer(o), device_id_type=MESH)

    def copy_z(other):
        return pltpu.make_async_remote_copy(
            src_ref=tiles_b.at[other], dst_ref=recv_z.at[zc],
            send_sem=sz.at[other], recv_sem=rz.at[zc], device_id=at_ring(other), device_id_type=MESH)

    def arrived_z(other):
        pltpu.make_async_remote_copy(
            src_ref=tiles_b.at[other], dst_ref=recv_z.at[other],
            send_sem=sz.at[other], recv_sem=rz.at[other], device_id=at_ring(other), device_id_type=MESH).wait_recv()

    def copy_y(block, o):
        to = lax.rem(yy + o, 4)
        return pltpu.make_async_remote_copy(
            src_ref=turned.at[block, to], dst_ref=recv_y.at[yy, block],
            send_sem=sy.at[block, o], recv_sem=ry.at[block, o], device_id=y_peer(o), device_id_type=MESH)

    @pl.loop(1, 32)
    def _(o):
        copy1(o).start()

    copy_z(z * 2 + 1 - core).start()

    @pl.loop(0, 12)
    def _(h):
        copy_z(far_z(h)).start()

    def add1(o, acc):
        copy1(o).wait_recv()
        return acc + recv1[o]

    total[0] = lax.fori_loop(1, 32, add1, part[pl.ds(mine, 8), :])

    @pl.loop(1, 16)
    def _(o):
        copy2(o).start()

    @pl.loop(12, 30)
    def _(h):
        copy_z(far_z(h)).start()

    recv_z[zc] = tiles_b[zc]

    def add2(o, acc):
        copy2(o).wait_recv()
        return acc + recv2[o]

    total[1] = lax.fori_loop(1, 16, add2, total[0])

    @pl.loop(1, 32)
    def _(o):
        copy3(o).start()

    priors[pl.ds(mine, 8), :] = total[1]

    @pl.loop(1, 32)
    def _(o):
        copy3(o).wait_recv()

    def forward(e):
        away = (e + 1) // 2
        block = lax.rem(z // 2 + (away if e % 2 else 8 - away), 8)
        if e == 0:
            @pl.loop(1, 4)
            def _(u):
                arrived_z(block * 4 + lax.rem(zc + u, 4))
        else:
            @pl.loop(0, 4)
            def _(u):
                arrived_z(block * 4 + u)
        four = [recv_z[block * 4 + j].astype(f32) for j in range(4)]
        four = exchange_four(four, 3, lanes)
        for j in range(4):
            turned[block, j] = four[j].astype(bf16)

        @pl.loop(1, 4)
        def _(o):
            copy_y(block, o).start()

        recv_y[yy, block] = turned[block, yy]

    cols = priors[...].T[:MEMBERS]
    mean = column_sum(cols) / MEMBERS
    anomaly = cols - mean
    members = lax.broadcasted_iota(jnp.int32, (MEMBERS, 128), 0)
    tiles = [anomaly[:, :128], anomaly[:, 128:], jnp.where(members == lanes, 1.0, 0.0).astype(f32)]
    means = [mean[:, :128], mean[:, 128:], jnp.zeros((1, 128), f32)]
    lane_row = lanes[:1]
    for batch in range(4):
        here = group_ref[batch]

        def away_from(other, here=here):
            return jnp.full((1, 128), jnp.abs(other - here), jnp.int32).astype(f32)

        if batch % 2 == 0:
            far = [jnp.where(lane_row < BATCH, 0.0, away_from(group_ref[batch + 1]))]
        else:
            far = [jnp.zeros((1, 128), f32)]
        if batch < 2:
            far.append(jnp.where(lane_row < BATCH, away_from(group_ref[2]), away_from(group_ref[3])))
        far.append(away_from(region))

        def chunk(c, carry, batch=batch, fixed=far[1:]):
            tiles, means, near, ahead = carry
            start = pl.multiple_of(batch * BATCH + c * CHUNK, CHUNK)
            block = [terms[i, pl.ds(start, CHUNK), :] for i in range(4)]
            for u in range(CHUNK):
                value, noise, root_noise, inverse_cut = [b[u:u + 1] for b in block]
                own, own_mean = ahead[0]
                raw = [(across_lanes(tiles[0], u + AHEAD), across_lanes(means[0], u + AHEAD))]
                gain, innovation = step_terms(own, own_mean, value, noise, root_noise)
                ahead_new = []
                for x, m in ahead[1:] + raw:
                    cov = column_sum(x * own)
                    ahead_new.append((x - own * (cov * gain), m + cov * innovation))
                ahead = ahead_new
                new_tiles, new_means = [], []
                for x, m, distance in zip(tiles, means, [near] + fixed):
                    cov = column_sum(x * own) * jnp.maximum(0.0, 1.0 - distance * inverse_cut)
                    new_tiles.append(x - own * (cov * gain))
                    new_means.append(m + cov * innovation)
                tiles, means = new_tiles, new_means
            tiles = [roll(tiles[0], -CHUNK)] + tiles[1:]
            means = [roll(means[0], -CHUNK)] + means[1:]
            return tiles, means, roll(near, -CHUNK), ahead

        ahead = [(across_lanes(tiles[0], j), across_lanes(means[0], j)) for j in range(AHEAD)]
        tiles, means, _, _ = lax.fori_loop(0, BATCH // CHUNK, chunk, (tiles, means, far[0], ahead))
        if batch % 2 == 1:
            tiles, means = tiles[1:], means[1:]
        forward(2 * batch)
        forward(2 * batch + 1)

    mixing = jnp.where(lanes < MEMBERS, tiles[0] + means[0], 0.0)
    rest = (1.0 - jnp.sum(mixing, axis=1, keepdims=True)) / MEMBERS
    mixing = (mixing + rest)[:, :MEMBERS]
    high = mixing.astype(bf16)
    low = (mixing - high.astype(f32)).astype(bf16)

    @pl.loop(0, 8)
    def _(block):
        @pl.loop(1, 4)
        def _(o):
            copy_y(block, o).wait_recv()

    @pl.loop(0, 8)
    def _(i):
        source = i // 2
        half = lax.rem(i, 2)
        four = []
        for j in range(4):
            block = recv_y[source, half * 4 + j]
            four.append(
                jnp.dot(high, block, preferred_element_type=f32)
                + jnp.dot(low, block, preferred_element_type=f32))
        four = exchange_four(four, 5, lanes)
        for level in range(4):
            out_ref[level, :, pl.ds(pl.multiple_of(i * 128, 128), 128)] = four[level].astype(bf16)

    copy_z(z * 2 + 1 - core).wait_send()

    @pl.loop(0, 30)
    def _(h):
        copy_z(far_z(h)).wait_send()

    @pl.loop(1, 32)
    def _(o):
        copy1(o).wait_send()
        copy3(o).wait_send()

    @pl.loop(1, 16)
    def _(o):
        copy2(o).wait_send()

    @pl.loop(0, 8)
    def _(block):
        @pl.loop(1, 4)
        def _(o):
            copy_y(block, o).wait_send()


def body(
    background_members,
    channel_height_kernel,
    sensor_spread_down,
    sensor_spread_across,
    measurement_placement,
    measurement_ordering,
    group_area_number,
    taper_radius_limit,
    measured_amounts,
    measurement_noise_spread,
):
    vmem = pl.BlockSpec(memory_space=pltpu.VMEM)
    smem = pl.BlockSpec(memory_space=pltpu.SMEM)
    dma = pltpu.SemaphoreType.DMA
    result = pl.pallas_call(
        kernel,
        out_shape=jax.ShapeDtypeStruct((4, MEMBERS, 1024), bf16),
        in_specs=[vmem] * 5 + [smem] * 5,
        out_specs=vmem,
        scratch_shapes=[
            pltpu.VMEM((32, 128), f32),
            pltpu.VMEM((MEMBERS * 32, 128), f32),
            pltpu.VMEM((32, MEMBERS, 128), f32),
            pltpu.VMEM((32, MEMBERS, 128), bf16),
            pltpu.VMEM((32, MEMBERS, 128), bf16),
            pltpu.VMEM((8, 4, MEMBERS, 128), bf16),
            pltpu.VMEM((4, 8, MEMBERS, 128), bf16),
            pltpu.VMEM((NOBS, 128), f32),
            pltpu.VMEM((2, 8, 128), f32),
            pltpu.VMEM((32, 8, 128), f32),
            pltpu.VMEM((16, 8, 128), f32),
            pltpu.VMEM((NOBS, 128), f32),
            pltpu.VMEM((4, NOBS, 128), f32),
            dma((32,)), dma((32,)), dma((16,)), dma((16,)), dma((32,)), dma((32,)),
            dma((32,)), dma((32,)), dma((8, 4)), dma((8, 4)),
        ],
        compiler_params=pltpu.CompilerParams(
            collective_id=0, has_side_effects=True, vmem_limit_bytes=62 * 1024 * 1024),
    )(
        background_members, measurement_placement, measurement_ordering, measured_amounts,
        measurement_noise_spread, channel_height_kernel.T, sensor_spread_down, sensor_spread_across,
        taper_radius_limit, group_area_number)
    return jnp.transpose(result, (1, 0, 2))[:, :, None, :]


def solution(mesh):
    return jax.shard_map(
        body,
        mesh=mesh,
        in_specs=(P(None, "lev", "region", None), P(None, "lev"), P(), P(), P(), P(), P(), P(), P(), P()),
        out_specs=P(None, "lev", "region", None),
        check_vma=False,
    )
```

```python
import jax
import jax.numpy as jnp
from jax import lax
from jax.experimental import pallas as pl
from jax.experimental.pallas import tpu as pltpu
from jax.sharding import PartitionSpec as P

MEMBERS = 80
NOBS = 256
BATCH = 64
CHUNK = 16
AHEAD = 3
RING = 32
MESH = pl.DeviceIdType.MESH
highest = lax.Precision.HIGHEST
f32 = jnp.float32
bf16 = jnp.bfloat16


def column_sum(x):
    return jnp.sum(x, axis=0, keepdims=True)


def roll(x, shift):
    return pltpu.roll(x, shift % 128, 1)


def exchange(low, high, bit, lanes):
    keep = (lanes // (1 << bit)) % 2 == 0
    return (
        jnp.where(keep, low, roll(high, 1 << bit)),
        jnp.where(keep, roll(low, -(1 << bit)), high),
    )


def exchange_four(tiles, bit, lanes):
    a, b, c, d = tiles
    a, b = exchange(a, b, bit, lanes)
    c, d = exchange(c, d, bit, lanes)
    a, c = exchange(a, c, bit + 1, lanes)
    b, d = exchange(b, d, bit + 1, lanes)
    return a, b, c, d


def across_lanes(x, lane):
    return jnp.broadcast_to(x[:, lane:lane + 1], (x.shape[0], 128))


def step_terms(own, own_mean, value, noise, root_noise):
    spread = column_sum(own * own) + noise
    root = lax.rsqrt(spread)
    gain = 1.0 / (spread + root_noise * (spread * root))
    return gain, (value - own_mean) * (root * root)


def kernel(
    x_ref, place_ref, order_ref, value_ref, noise_ref,
    height_ref, down_ref, across_ref, limit_ref, group_ref, out_ref,
    table, flat, tiles_f, tiles_b, recv_z, turned, recv_y,
    part, total, recv1, recv2, priors, terms,
    halves, s1, r1, s2, r2, s3, r3, s4, r4, sz, rz, sy, ry,
):
    region = lax.axis_index("region")
    lev = lax.axis_index("lev")
    yy = region // RING
    zc = lax.rem(region, RING)
    z = zc // 2
    core = lax.rem(zc, 2)
    slab = lev * 4 + yy

    def slab_peer(o):
        g = lax.rem(slab + o, 16)
        return (lax.rem(g, 4) * RING + zc, g // 4)

    def far_z(h):
        e = h // 2
        size = e // 2 + 1
        dz = size + lax.rem(e, 2) * (16 - 2 * size)
        return lax.rem(z + dz, 16) * 2 + lax.rem(h, 2)

    def at_ring(other):
        return (yy * RING + other, lev)

    def line_peer(o):
        return (yy * RING + lax.rem(z + o, 16) * 2 + core, lev)

    def y_peer(o):
        return (lax.rem(yy + o, 4) * RING + zc, lev)

    barrier = pltpu.get_barrier_semaphore()

    partner = (yy * RING + z * 2 + 1 - core, lev)
    pl.semaphore_signal(barrier, inc=1, device_id=partner, device_id_type=MESH)

    @pl.loop(1, 16)
    def _(o):
        pl.semaphore_signal(barrier, inc=1, device_id=slab_peer(o), device_id_type=MESH)

    @pl.loop(0, 30)
    def _(h):
        pl.semaphore_signal(barrier, inc=1, device_id=at_ring(far_z(h)), device_id_type=MESH)

    lanes = lax.broadcasted_iota(jnp.int32, (MEMBERS, 128), 1)

    flat[...] = x_ref[...].astype(f32).reshape(MEMBERS * 32, 128)
    swapped = ((lanes // 8) % 4) * 32 + (lanes // 32) * 8 + lanes % 8
    wanted = jnp.full((MEMBERS, 128), group_ref[0], jnp.int32)
    for k in range(1, 4):
        wanted = jnp.where(lanes // 32 == k, group_ref[k], wanted)

    def first_pass(q, seen):
        four = []
        for j in range(4):
            tile = flat[pl.ds(q * 4 + j, MEMBERS, stride=32), :]
            seen = jnp.where(lanes % 32 == q * 4 + j, jnp.take_along_axis(tile, wanted, axis=1), seen)
            four.append(jnp.take_along_axis(tile, swapped, axis=1))
        four = exchange_four(four, 0, lanes)
        for j in range(4):
            tiles_f[q * 4 + j] = four[j]
        return seen

    seen = lax.fori_loop(0, 8, first_pass, jnp.zeros((MEMBERS, 128), f32))

    table[...] = jnp.zeros_like(table)
    table[0:4, 0:BATCH] = place_ref[...].astype(f32)
    table[8:12, 0:BATCH] = order_ref[...].astype(f32)
    table[16:20, 0:BATCH] = value_ref[...]
    table[24:28, 0:BATCH] = noise_ref[...]
    orders = table[8:16, :].T
    wide = lax.broadcasted_iota(jnp.int32, (BATCH, 128), 1)
    wide_f = wide.astype(f32)
    row_block = (region // 16).astype(f32)
    lane_column = (lax.rem(region, 4) * 2 + (wide % 8) // 4).astype(f32)
    lane_batch = wide // 32
    wide_row = wide[:1]
    down_here = jnp.float32(0.0)
    foot = jnp.zeros((1, 128), f32)
    for i in range(4):
        down_here = jnp.where(lax.rem(region // 4, 4) == i, down_ref[i], down_here)
        foot = jnp.where(wide_row % 4 == i, across_ref[i], foot)
    foot = foot * down_here
    heights = []
    for c in range(8):
        row = jnp.zeros((1, 128), f32)
        for l in range(4):
            row = jnp.where((wide_row // 8) % 4 == l, height_ref[l, c], row)
        heights.append(row)
    weights = []
    for k in range(4):
        order = orders[:BATCH, k:k + 1] == wide_f

        def ordered(row, order=order):
            return jnp.sum(jnp.where(order, table[row:row + 1, :], 0.0), axis=1, keepdims=True)

        picked = ordered(k)
        value = ordered(16 + k)
        noise = ordered(24 + k) * 79.0
        channel = jnp.floor(picked * (1.0 / 64.0))
        site = picked - channel * 64.0
        down = jnp.floor(site * 0.125)
        along = site - down * 8.0
        cut = jnp.zeros((BATCH, 1), f32)
        height = jnp.zeros((BATCH, 128), f32)
        for c in range(8):
            here = channel == float(c)
            cut = jnp.where(here, limit_ref[c].astype(f32), cut)
            height = jnp.where(here, heights[c], height)
        hit = (down == row_block) & (along == lane_column) & (lane_batch == k)
        weights.append(jnp.where(hit, height * foot, 0.0))
        rows = pl.ds(k * BATCH, BATCH)
        terms[0, rows, :] = jnp.broadcast_to(value, (BATCH, 128))
        terms[1, rows, :] = jnp.broadcast_to(noise, (BATCH, 128))
        terms[2, rows, :] = jnp.broadcast_to(jnp.sqrt(noise), (BATCH, 128))
        terms[3, rows, :] = jnp.broadcast_to(1.0 / (cut + 1.0), (BATCH, 128))

    part[...] = jnp.zeros_like(part)
    part[:, :MEMBERS] = lax.dot_general(
        jnp.concatenate(weights), seen, (((1,), (1,)), ((), ())),
        precision=highest, preferred_element_type=f32)

    @pl.loop(0, 8, unroll=2)
    def _(q):
        four = exchange_four([tiles_f[q + 8 * j] for j in range(4)], 5, lanes)
        for j in range(4):
            tiles_f[q + 8 * j] = four[j]

    @pl.loop(0, 16, unroll=4)
    def _(q):
        low = (q // 4) * 8 + lax.rem(q, 4)
        a, b = exchange(tiles_f[low], tiles_f[low + 4], 2, lanes)
        tiles_b[low] = a.astype(bf16)
        tiles_b[low + 4] = b.astype(bf16)

    pl.semaphore_wait(barrier, 46)

    def copy1(o):
        row = pl.multiple_of(lax.rem(slab + o, 16) * 8, 8)
        return pltpu.make_async_remote_copy(
            src_ref=halves.at[1, pl.ds(row, 8)], dst_ref=recv1.at[o],
            send_sem=s1.at[o], recv_sem=r1.at[o], device_id=slab_peer(o), device_id_type=MESH)

    def copy2(o):
        return pltpu.make_async_remote_copy(
            src_ref=total.at[0], dst_ref=recv2.at[o],
            send_sem=s2.at[o], recv_sem=r2.at[o], device_id=line_peer(o), device_id_type=MESH)

    mine = pl.multiple_of(slab * 8, 8)
    kept = pl.multiple_of(core * 128, 128)
    given = pl.multiple_of(128 - core * 128, 128)
    placed = pl.multiple_of(core * 128 + slab * 8, 8)
    to_partner = pltpu.make_async_remote_copy(
        src_ref=part.at[pl.ds(given, 128)], dst_ref=halves.at[0],
        send_sem=s4.at[0], recv_sem=r4.at[0], device_id=partner, device_id_type=MESH)
    back_to_partner = pltpu.make_async_remote_copy(
        src_ref=priors.at[pl.ds(kept, 128)], dst_ref=priors.at[pl.ds(kept, 128)],
        send_sem=s4.at[1], recv_sem=r4.at[1], device_id=partner, device_id_type=MESH)

    def copy3(o):
        return pltpu.make_async_remote_copy(
            src_ref=total.at[1], dst_ref=priors.at[pl.ds(placed, 8)],
            send_sem=s3.at[o], recv_sem=r3.at[o], device_id=slab_peer(o), device_id_type=MESH)

    def copy_z(other):
        return pltpu.make_async_remote_copy(
            src_ref=tiles_b.at[other], dst_ref=recv_z.at[zc],
            send_sem=sz.at[other], recv_sem=rz.at[zc], device_id=at_ring(other), device_id_type=MESH)

    def arrived_z(other):
        pltpu.make_async_remote_copy(
            src_ref=tiles_b.at[other], dst_ref=recv_z.at[other],
            send_sem=sz.at[other], recv_sem=rz.at[other], device_id=at_ring(other), device_id_type=MESH).wait_recv()

    def copy_y(block, o):
        to = lax.rem(yy + o, 4)
        return pltpu.make_async_remote_copy(
            src_ref=turned.at[block, to], dst_ref=recv_y.at[yy, block],
            send_sem=sy.at[block, o], recv_sem=ry.at[block, o], device_id=y_peer(o), device_id_type=MESH)

    to_partner.start()
    to_partner.wait_recv()
    halves[1] = part[pl.ds(kept, 128), :] + halves[0]

    @pl.loop(1, 16)
    def _(o):
        copy1(o).start()

    copy_z(z * 2 + 1 - core).start()

    @pl.loop(0, 12)
    def _(h):
        copy_z(far_z(h)).start()

    def add1(o, acc):
        copy1(o).wait_recv()
        return acc + recv1[o]

    total[0] = lax.fori_loop(1, 16, add1, halves[1, pl.ds(mine, 8), :])

    @pl.loop(1, 16)
    def _(o):
        copy2(o).start()

    @pl.loop(12, 20)
    def _(h):
        copy_z(far_z(h)).start()

    recv_z[zc] = tiles_b[zc]

    def add2(o, acc):
        copy2(o).wait_recv()
        return acc + recv2[o]

    total[1] = lax.fori_loop(1, 16, add2, total[0])

    @pl.loop(1, 16)
    def _(o):
        copy3(o).start()

    @pl.loop(20, 30)
    def _(h):
        copy_z(far_z(h)).start()

    priors[pl.ds(placed, 8), :] = total[1]

    @pl.loop(1, 16)
    def _(o):
        copy3(o).wait_recv()

    back_to_partner.start()
    back_to_partner.wait_recv()

    def forward(e, first=False):
        away = (e + 1) // 2
        block = lax.rem(z // 2 + away + lax.rem(e + 1, 2) * (8 - 2 * away), 8)

        @pl.loop(1 if first else 0, 4)
        def _(u):
            arrived_z(block * 4 + (lax.rem(zc + u, 4) if first else u))

        four = [recv_z[block * 4 + j].astype(f32) for j in range(4)]
        four = exchange_four(four, 3, lanes)
        for j in range(4):
            turned[block, j] = four[j].astype(bf16)

        @pl.loop(1, 4)
        def _(o):
            copy_y(block, o).start()

        recv_y[yy, block] = turned[block, yy]

    cols = priors[...].T[:MEMBERS]
    mean = column_sum(cols) / MEMBERS
    anomaly = cols - mean
    members = lax.broadcasted_iota(jnp.int32, (MEMBERS, 128), 0)
    tiles = [anomaly[:, :128], anomaly[:, 128:], jnp.where(members == lanes, 1.0, 0.0).astype(f32)]
    means = [mean[:, :128], mean[:, 128:], jnp.zeros((1, 128), f32)]
    lane_row = lanes[:1]
    forward(0, first=True)
    for half in range(2):

        def one_batch(part, carry, half=half):
            tiles, means = carry
            batch = half * 2 + part
            here = group_ref[batch]

            def away_from(other):
                return jnp.full((1, 128), jnp.abs(other - here), jnp.int32).astype(f32)

            near = jnp.where(lane_row < BATCH, 0.0, away_from(group_ref[half * 2 + 1]))
            fixed = [away_from(region)]
            if half == 0:
                fixed = [jnp.where(lane_row < BATCH, away_from(group_ref[2]), away_from(group_ref[3]))] + fixed

            def chunk(c, carry):
                tiles, means, near, ahead = carry
                start = pl.multiple_of(batch * BATCH + c * CHUNK, CHUNK)
                block = [terms[i, pl.ds(start, CHUNK), :] for i in range(4)]
                for u in range(CHUNK):
                    value, noise, root_noise, inverse_cut = [b[u:u + 1] for b in block]
                    own, own_mean = ahead[0]
                    raw = [(across_lanes(tiles[0], u + AHEAD), across_lanes(means[0], u + AHEAD))]
                    gain, innovation = step_terms(own, own_mean, value, noise, root_noise)
                    ahead_new = []
                    for x, m in ahead[1:] + raw:
                        cov = column_sum(x * own)
                        ahead_new.append((x - own * (cov * gain), m + cov * innovation))
                    ahead = ahead_new
                    new_tiles, new_means = [], []
                    for x, m, distance in zip(tiles, means, [near] + fixed):
                        cov = column_sum(x * own) * jnp.maximum(0.0, 1.0 - distance * inverse_cut)
                        new_tiles.append(x - own * (cov * gain))
                        new_means.append(m + cov * innovation)
                    tiles, means = new_tiles, new_means
                tiles = [roll(tiles[0], -CHUNK)] + tiles[1:]
                means = [roll(means[0], -CHUNK)] + means[1:]
                return tiles, means, roll(near, -CHUNK), ahead

            ahead = [(across_lanes(tiles[0], j), across_lanes(means[0], j)) for j in range(AHEAD)]
            tiles, means, _, _ = lax.fori_loop(0, BATCH // CHUNK, chunk, (tiles, means, near, ahead))

            @pl.loop(2 * batch + 1, jnp.minimum(2 * batch + 3, 8))
            def _(e):
                forward(e)

            return tiles, means

        tiles, means = lax.fori_loop(0, 2, one_batch, (tiles, means))
        tiles, means = tiles[1:], means[1:]

    mixing = jnp.where(lanes < MEMBERS, tiles[0] + means[0], 0.0)
    rest = (1.0 - jnp.sum(mixing, axis=1, keepdims=True)) / MEMBERS
    mixing = (mixing + rest)[:, :MEMBERS]
    high = mixing.astype(bf16)
    low = (mixing - high.astype(f32)).astype(bf16)
    both = jnp.concatenate([high, low])

    @pl.loop(0, 8)
    def _(i):
        half = lax.rem(z // 8 + i // 4, 2)
        source = lax.rem(i, 4)

        @pl.when(source == 0)
        def _():
            @pl.loop(0, 12)
            def _(n):
                copy_y(half * 4 + n // 3, 1 + lax.rem(n, 3)).wait_recv()

        blocks = jnp.concatenate([recv_y[source, half * 4 + j] for j in range(4)], axis=1)
        mixed = jnp.dot(both, blocks, preferred_element_type=f32)
        mixed = mixed[:MEMBERS] + mixed[MEMBERS:]
        four = [mixed[:, j * 128:(j + 1) * 128] for j in range(4)]
        four = exchange_four(four, 5, lanes)
        for level in range(4):
            out_ref[level, :, pl.ds(pl.multiple_of((source * 2 + half) * 128, 128), 128)] = four[level].astype(bf16)

    copy_z(z * 2 + 1 - core).wait_send()

    @pl.loop(0, 30)
    def _(h):
        copy_z(far_z(h)).wait_send()

    to_partner.wait_send()
    back_to_partner.wait_send()

    @pl.loop(1, 16)
    def _(o):
        copy1(o).wait_send()
        copy3(o).wait_send()

    @pl.loop(1, 16)
    def _(o):
        copy2(o).wait_send()

    @pl.loop(0, 8)
    def _(block):
        @pl.loop(1, 4)
        def _(o):
            copy_y(block, o).wait_send()


def body(
    background_members,
    channel_height_kernel,
    sensor_spread_down,
    sensor_spread_across,
    measurement_placement,
    measurement_ordering,
    group_area_number,
    taper_radius_limit,
    measured_amounts,
    measurement_noise_spread,
):
    vmem = pl.BlockSpec(memory_space=pltpu.VMEM)
    smem = pl.BlockSpec(memory_space=pltpu.SMEM)
    dma = pltpu.SemaphoreType.DMA
    result = pl.pallas_call(
        kernel,
        out_shape=jax.ShapeDtypeStruct((4, MEMBERS, 1024), bf16),
        in_specs=[vmem] * 5 + [smem] * 5,
        out_specs=vmem,
        scratch_shapes=[
            pltpu.VMEM((32, 128), f32),
            pltpu.VMEM((MEMBERS * 32, 128), f32),
            pltpu.VMEM((32, MEMBERS, 128), f32),
            pltpu.VMEM((32, MEMBERS, 128), bf16),
            pltpu.VMEM((32, MEMBERS, 128), bf16),
            pltpu.VMEM((8, 4, MEMBERS, 128), bf16),
            pltpu.VMEM((4, 8, MEMBERS, 128), bf16),
            pltpu.VMEM((NOBS, 128), f32),
            pltpu.VMEM((2, 8, 128), f32),
            pltpu.VMEM((16, 8, 128), f32),
            pltpu.VMEM((16, 8, 128), f32),
            pltpu.VMEM((NOBS, 128), f32),
            pltpu.VMEM((4, NOBS, 128), f32),
            pltpu.VMEM((2, 128, 128), f32),
            dma((16,)), dma((16,)), dma((16,)), dma((16,)), dma((16,)), dma((16,)),
            dma((2,)), dma((2,)), dma((32,)), dma((32,)), dma((8, 4)), dma((8, 4)),
        ],
        compiler_params=pltpu.CompilerParams(
            collective_id=0, has_side_effects=True, vmem_limit_bytes=62 * 1024 * 1024),
    )(
        background_members, measurement_placement, measurement_ordering, measured_amounts,
        measurement_noise_spread, channel_height_kernel.T, sensor_spread_down, sensor_spread_across,
        taper_radius_limit, group_area_number)
    return jnp.transpose(result, (1, 0, 2))[:, :, None, :]


def solution(mesh):
    return jax.shard_map(
        body,
        mesh=mesh,
        in_specs=(P(None, "lev", "region", None), P(None, "lev"), P(), P(), P(), P(), P(), P(), P(), P()),
        out_specs=P(None, "lev", "region", None),
        check_vma=False,
    )
```

```python
import jax
import jax.numpy as jnp
from jax import lax
from jax.experimental import pallas as pl
from jax.experimental.pallas import tpu as pltpu
from jax.sharding import PartitionSpec as P

MEMBERS = 80
NOBS = 256
BATCH = 64
CHUNK = 16
AHEAD = 3
RING = 32
MESH = pl.DeviceIdType.MESH
highest = lax.Precision.HIGHEST
f32 = jnp.float32
bf16 = jnp.bfloat16


def column_sum(x):
    return jnp.sum(x, axis=0, keepdims=True)


def roll(x, shift):
    return pltpu.roll(x, shift % 128, 1)


def exchange(low, high, bit, lanes):
    keep = (lanes // (1 << bit)) % 2 == 0
    return (
        jnp.where(keep, low, roll(high, 1 << bit)),
        jnp.where(keep, roll(low, -(1 << bit)), high),
    )


def exchange_four(tiles, bit, lanes):
    a, b, c, d = tiles
    a, b = exchange(a, b, bit, lanes)
    c, d = exchange(c, d, bit, lanes)
    a, c = exchange(a, c, bit + 1, lanes)
    b, d = exchange(b, d, bit + 1, lanes)
    return a, b, c, d


def across_lanes(x, lane):
    return jnp.broadcast_to(x[:, lane:lane + 1], (x.shape[0], 128))


def step_terms(own, own_mean, value, noise, root_noise):
    spread = column_sum(own * own) + noise
    root = lax.rsqrt(spread)
    gain = 1.0 / (spread + root_noise * (spread * root))
    return gain, (value - own_mean) * (root * root)


def kernel(
    x_ref, place_ref, order_ref, value_ref, noise_ref,
    height_ref, down_ref, across_ref, limit_ref, group_ref, out_ref,
    table, flat, tiles_f, tiles_b, recv_z, turned, recv_y,
    part, total, recv1, recv2, priors, terms,
    halves, s1, r1, s2, r2, s3, r3, s4, r4, sz, rz, sy, ry,
):
    region = lax.axis_index("region")
    lev = lax.axis_index("lev")
    yy = region // RING
    zc = lax.rem(region, RING)
    z = zc // 2
    core = lax.rem(zc, 2)
    slab = lev * 4 + yy

    def slab_peer(o):
        g = lax.rem(slab + o, 16)
        return (lax.rem(g, 4) * RING + zc, g // 4)

    def far_z(h):
        e = h // 2
        size = e // 2 + 1
        dz = size + lax.rem(e, 2) * (16 - 2 * size)
        return lax.rem(z + dz, 16) * 2 + lax.rem(h, 2)

    def at_ring(other):
        return (yy * RING + other, lev)

    def line_peer(o):
        return (yy * RING + lax.rem(z + o, 16) * 2 + core, lev)

    def y_peer(o):
        return (lax.rem(yy + o, 4) * RING + zc, lev)

    barrier = pltpu.get_barrier_semaphore()

    partner = (yy * RING + z * 2 + 1 - core, lev)
    pl.semaphore_signal(barrier, inc=1, device_id=partner, device_id_type=MESH)

    @pl.loop(1, 16)
    def _(o):
        pl.semaphore_signal(barrier, inc=1, device_id=slab_peer(o), device_id_type=MESH)

    @pl.loop(0, 30)
    def _(h):
        pl.semaphore_signal(barrier, inc=1, device_id=at_ring(far_z(h)), device_id_type=MESH)

    lanes = lax.broadcasted_iota(jnp.int32, (MEMBERS, 128), 1)

    flat[...] = x_ref[...].astype(f32).reshape(MEMBERS * 32, 128)
    swapped = ((lanes // 8) % 4) * 32 + (lanes // 32) * 8 + lanes % 8
    wanted = jnp.full((MEMBERS, 128), group_ref[0], jnp.int32)
    for k in range(1, 4):
        wanted = jnp.where(lanes // 32 == k, group_ref[k], wanted)

    def first_pass(q, seen):
        four = []
        for j in range(4):
            tile = flat[pl.ds(q * 4 + j, MEMBERS, stride=32), :]
            seen = jnp.where(lanes % 32 == q * 4 + j, jnp.take_along_axis(tile, wanted, axis=1), seen)
            four.append(jnp.take_along_axis(tile, swapped, axis=1))
        four = exchange_four(four, 0, lanes)
        for j in range(4):
            tiles_f[q * 4 + j] = four[j]
        return seen

    seen = lax.fori_loop(0, 8, first_pass, jnp.zeros((MEMBERS, 128), f32))

    table[...] = jnp.zeros_like(table)
    table[0:4, 0:BATCH] = place_ref[...].astype(f32)
    table[8:12, 0:BATCH] = order_ref[...].astype(f32)
    table[16:20, 0:BATCH] = value_ref[...]
    table[24:28, 0:BATCH] = noise_ref[...]
    orders = table[8:16, :].T
    wide = lax.broadcasted_iota(jnp.int32, (BATCH, 128), 1)
    wide_f = wide.astype(f32)
    row_block = (region // 16).astype(f32)
    lane_column = (lax.rem(region, 4) * 2 + (wide % 8) // 4).astype(f32)
    lane_batch = wide // 32
    wide_row = wide[:1]
    down_here = jnp.float32(0.0)
    foot = jnp.zeros((1, 128), f32)
    for i in range(4):
        down_here = jnp.where(lax.rem(region // 4, 4) == i, down_ref[i], down_here)
        foot = jnp.where(wide_row % 4 == i, across_ref[i], foot)
    foot = foot * down_here
    heights = []
    for c in range(8):
        row = jnp.zeros((1, 128), f32)
        for l in range(4):
            row = jnp.where((wide_row // 8) % 4 == l, height_ref[l, c], row)
        heights.append(row)
    weights = []
    for k in range(4):
        order = orders[:BATCH, k:k + 1] == wide_f

        def ordered(row, order=order):
            return jnp.sum(jnp.where(order, table[row:row + 1, :], 0.0), axis=1, keepdims=True)

        picked = ordered(k)
        value = ordered(16 + k)
        noise = ordered(24 + k) * 79.0
        channel = jnp.floor(picked * (1.0 / 64.0))
        site = picked - channel * 64.0
        down = jnp.floor(site * 0.125)
        along = site - down * 8.0
        cut = jnp.zeros((BATCH, 1), f32)
        height = jnp.zeros((BATCH, 128), f32)
        for c in range(8):
            here = channel == float(c)
            cut = jnp.where(here, limit_ref[c].astype(f32), cut)
            height = jnp.where(here, heights[c], height)
        hit = (down == row_block) & (along == lane_column) & (lane_batch == k)
        weights.append(jnp.where(hit, height * foot, 0.0))
        rows = pl.ds(k * BATCH, BATCH)
        terms[0, rows, :] = jnp.broadcast_to(value, (BATCH, 128))
        terms[1, rows, :] = jnp.broadcast_to(noise, (BATCH, 128))
        terms[2, rows, :] = jnp.broadcast_to(jnp.sqrt(noise), (BATCH, 128))
        terms[3, rows, :] = jnp.broadcast_to(1.0 / (cut + 1.0), (BATCH, 128))

    part[...] = jnp.zeros_like(part)
    part[:, :MEMBERS] = lax.dot_general(
        jnp.concatenate(weights), seen, (((1,), (1,)), ((), ())),
        precision=highest, preferred_element_type=f32)

    @pl.loop(0, 8, unroll=2)
    def _(q):
        four = exchange_four([tiles_f[q + 8 * j] for j in range(4)], 5, lanes)
        for j in range(4):
            tiles_f[q + 8 * j] = four[j]

    @pl.loop(0, 16, unroll=4)
    def _(q):
        low = (q // 4) * 8 + lax.rem(q, 4)
        a, b = exchange(tiles_f[low], tiles_f[low + 4], 2, lanes)
        tiles_b[low] = a.astype(bf16)
        tiles_b[low + 4] = b.astype(bf16)

    pl.semaphore_wait(barrier, 46)

    def copy1(o):
        row = pl.multiple_of(lax.rem(slab + o, 16) * 8, 8)
        return pltpu.make_async_remote_copy(
            src_ref=halves.at[1, pl.ds(row, 8)], dst_ref=recv1.at[o],
            send_sem=s1.at[o], recv_sem=r1.at[o], device_id=slab_peer(o), device_id_type=MESH)

    def copy2(o):
        return pltpu.make_async_remote_copy(
            src_ref=total.at[0], dst_ref=recv2.at[o],
            send_sem=s2.at[o], recv_sem=r2.at[o], device_id=line_peer(o), device_id_type=MESH)

    mine = pl.multiple_of(slab * 8, 8)
    kept = pl.multiple_of(core * 128, 128)
    given = pl.multiple_of(128 - core * 128, 128)
    placed = pl.multiple_of(core * 128 + slab * 8, 8)
    to_partner = pltpu.make_async_remote_copy(
        src_ref=part.at[pl.ds(given, 128)], dst_ref=halves.at[0],
        send_sem=s4.at[0], recv_sem=r4.at[0], device_id=partner, device_id_type=MESH)
    back_to_partner = pltpu.make_async_remote_copy(
        src_ref=priors.at[pl.ds(kept, 128)], dst_ref=priors.at[pl.ds(kept, 128)],
        send_sem=s4.at[1], recv_sem=r4.at[1], device_id=partner, device_id_type=MESH)

    def copy3(o):
        return pltpu.make_async_remote_copy(
            src_ref=total.at[1], dst_ref=priors.at[pl.ds(placed, 8)],
            send_sem=s3.at[o], recv_sem=r3.at[o], device_id=slab_peer(o), device_id_type=MESH)

    def copy_z(other):
        return pltpu.make_async_remote_copy(
            src_ref=tiles_b.at[other], dst_ref=recv_z.at[zc],
            send_sem=sz.at[other], recv_sem=rz.at[zc], device_id=at_ring(other), device_id_type=MESH)

    def arrived_z(other):
        pltpu.make_async_remote_copy(
            src_ref=tiles_b.at[other], dst_ref=recv_z.at[other],
            send_sem=sz.at[other], recv_sem=rz.at[other], device_id=at_ring(other), device_id_type=MESH).wait_recv()

    def copy_y(block, o):
        to = lax.rem(yy + o, 4)
        return pltpu.make_async_remote_copy(
            src_ref=turned.at[block, to], dst_ref=recv_y.at[yy, block],
            send_sem=sy.at[block, o], recv_sem=ry.at[block, o], device_id=y_peer(o), device_id_type=MESH)

    to_partner.start()
    copy_z(z * 2 + 1 - core).start()

    @pl.loop(0, 8)
    def _(h):
        copy_z(far_z(h)).start()

    to_partner.wait_recv()
    halves[1] = part[pl.ds(kept, 128), :] + halves[0]

    @pl.loop(1, 16)
    def _(o):
        copy1(o).start()

    def add1(o, acc):
        copy1(o).wait_recv()
        return acc + recv1[o]

    total[0] = lax.fori_loop(1, 16, add1, halves[1, pl.ds(mine, 8), :])

    @pl.loop(1, 16)
    def _(o):
        copy2(o).start()

    @pl.loop(8, 18)
    def _(h):
        copy_z(far_z(h)).start()

    recv_z[zc] = tiles_b[zc]

    def add2(o, acc):
        copy2(o).wait_recv()
        return acc + recv2[o]

    total[1] = lax.fori_loop(1, 16, add2, total[0])

    @pl.loop(1, 16)
    def _(o):
        copy3(o).start()

    @pl.loop(18, 30)
    def _(h):
        copy_z(far_z(h)).start()

    priors[pl.ds(placed, 8), :] = total[1]

    @pl.loop(1, 16)
    def _(o):
        copy3(o).wait_recv()

    back_to_partner.start()
    back_to_partner.wait_recv()

    def forward(e, first=False):
        away = (e + 1) // 2
        block = lax.rem(z // 2 + away + lax.rem(e + 1, 2) * (8 - 2 * away), 8)

        @pl.loop(1 if first else 0, 4)
        def _(u):
            arrived_z(block * 4 + (lax.rem(zc + u, 4) if first else u))

        four = [recv_z[block * 4 + j].astype(f32) for j in range(4)]
        four = exchange_four(four, 3, lanes)
        for j in range(4):
            turned[block, j] = four[j].astype(bf16)

        @pl.loop(1, 4)
        def _(o):
            copy_y(block, o).start()

        recv_y[yy, block] = turned[block, yy]

    cols = priors[...].T[:MEMBERS]
    mean = column_sum(cols) / MEMBERS
    anomaly = cols - mean
    members = lax.broadcasted_iota(jnp.int32, (MEMBERS, 128), 0)
    tiles = [anomaly[:, :128], anomaly[:, 128:], jnp.where(members == lanes, 1.0, 0.0).astype(f32)]
    means = [mean[:, :128], mean[:, 128:], jnp.zeros((1, 128), f32)]
    lane_row = lanes[:1]
    forward(0, first=True)
    for half in range(2):

        def one_batch(part, carry, half=half):
            tiles, means = carry
            batch = half * 2 + part
            here = group_ref[batch]

            def away_from(other):
                return jnp.full((1, 128), jnp.abs(other - here), jnp.int32).astype(f32)

            near = jnp.where(lane_row < BATCH, 0.0, away_from(group_ref[half * 2 + 1]))
            fixed = [away_from(region)]
            if half == 0:
                fixed = [jnp.where(lane_row < BATCH, away_from(group_ref[2]), away_from(group_ref[3]))] + fixed

            def chunk(c, carry):
                tiles, means, near, ahead = carry
                start = pl.multiple_of(batch * BATCH + c * CHUNK, CHUNK)
                block = [terms[i, pl.ds(start, CHUNK), :] for i in range(4)]
                for u in range(CHUNK):
                    value, noise, root_noise, inverse_cut = [b[u:u + 1] for b in block]
                    own, own_mean = ahead[0]
                    raw = [(across_lanes(tiles[0], u + AHEAD), across_lanes(means[0], u + AHEAD))]
                    gain, innovation = step_terms(own, own_mean, value, noise, root_noise)
                    ahead_new = []
                    for x, m in ahead[1:] + raw:
                        cov = column_sum(x * own)
                        ahead_new.append((x - own * (cov * gain), m + cov * innovation))
                    ahead = ahead_new
                    new_tiles, new_means = [], []
                    for x, m, distance in zip(tiles, means, [near] + fixed):
                        cov = column_sum(x * own) * jnp.maximum(0.0, 1.0 - distance * inverse_cut)
                        new_tiles.append(x - own * (cov * gain))
                        new_means.append(m + cov * innovation)
                    tiles, means = new_tiles, new_means
                tiles = [roll(tiles[0], -CHUNK)] + tiles[1:]
                means = [roll(means[0], -CHUNK)] + means[1:]
                return tiles, means, roll(near, -CHUNK), ahead

            ahead = [(across_lanes(tiles[0], j), across_lanes(means[0], j)) for j in range(AHEAD)]
            tiles, means, _, _ = lax.fori_loop(0, BATCH // CHUNK, chunk, (tiles, means, near, ahead))

            @pl.loop(2 * batch + 1, jnp.minimum(2 * batch + 3, 8))
            def _(e):
                forward(e)

            return tiles, means

        tiles, means = lax.fori_loop(0, 2, one_batch, (tiles, means))
        tiles, means = tiles[1:], means[1:]

    mixing = jnp.where(lanes < MEMBERS, tiles[0] + means[0], 0.0)
    rest = (1.0 - jnp.sum(mixing, axis=1, keepdims=True)) / MEMBERS
    mixing = (mixing + rest)[:, :MEMBERS]
    high = mixing.astype(bf16)
    low = (mixing - high.astype(f32)).astype(bf16)
    both = jnp.concatenate([high, low])

    @pl.loop(0, 8)
    def _(i):
        half = lax.rem(z // 8 + i // 4, 2)
        source = lax.rem(i, 4)

        @pl.when(source == 0)
        def _():
            @pl.loop(0, 12)
            def _(n):
                copy_y(half * 4 + n // 3, 1 + lax.rem(n, 3)).wait_recv()

        blocks = jnp.concatenate([recv_y[source, half * 4 + j] for j in range(4)], axis=1)
        mixed = jnp.dot(both, blocks, preferred_element_type=f32)
        mixed = mixed[:MEMBERS] + mixed[MEMBERS:]
        four = [mixed[:, j * 128:(j + 1) * 128] for j in range(4)]
        four = exchange_four(four, 5, lanes)
        for level in range(4):
            out_ref[level, :, pl.ds(pl.multiple_of((source * 2 + half) * 128, 128), 128)] = four[level].astype(bf16)

    copy_z(z * 2 + 1 - core).wait_send()

    @pl.loop(0, 30)
    def _(h):
        copy_z(far_z(h)).wait_send()

    to_partner.wait_send()
    back_to_partner.wait_send()

    @pl.loop(1, 16)
    def _(o):
        copy1(o).wait_send()
        copy3(o).wait_send()

    @pl.loop(1, 16)
    def _(o):
        copy2(o).wait_send()

    @pl.loop(0, 8)
    def _(block):
        @pl.loop(1, 4)
        def _(o):
            copy_y(block, o).wait_send()


def body(
    background_members,
    channel_height_kernel,
    sensor_spread_down,
    sensor_spread_across,
    measurement_placement,
    measurement_ordering,
    group_area_number,
    taper_radius_limit,
    measured_amounts,
    measurement_noise_spread,
):
    vmem = pl.BlockSpec(memory_space=pltpu.VMEM)
    smem = pl.BlockSpec(memory_space=pltpu.SMEM)
    dma = pltpu.SemaphoreType.DMA
    result = pl.pallas_call(
        kernel,
        out_shape=jax.ShapeDtypeStruct((4, MEMBERS, 1024), bf16),
        in_specs=[vmem] * 5 + [smem] * 5,
        out_specs=vmem,
        scratch_shapes=[
            pltpu.VMEM((32, 128), f32),
            pltpu.VMEM((MEMBERS * 32, 128), f32),
            pltpu.VMEM((32, MEMBERS, 128), f32),
            pltpu.VMEM((32, MEMBERS, 128), bf16),
            pltpu.VMEM((32, MEMBERS, 128), bf16),
            pltpu.VMEM((8, 4, MEMBERS, 128), bf16),
            pltpu.VMEM((4, 8, MEMBERS, 128), bf16),
            pltpu.VMEM((NOBS, 128), f32),
            pltpu.VMEM((2, 8, 128), f32),
            pltpu.VMEM((16, 8, 128), f32),
            pltpu.VMEM((16, 8, 128), f32),
            pltpu.VMEM((NOBS, 128), f32),
            pltpu.VMEM((4, NOBS, 128), f32),
            pltpu.VMEM((2, 128, 128), f32),
            dma((16,)), dma((16,)), dma((16,)), dma((16,)), dma((16,)), dma((16,)),
            dma((2,)), dma((2,)), dma((32,)), dma((32,)), dma((8, 4)), dma((8, 4)),
        ],
        compiler_params=pltpu.CompilerParams(
            collective_id=0, has_side_effects=True, vmem_limit_bytes=62 * 1024 * 1024),
    )(
        background_members, measurement_placement, measurement_ordering, measured_amounts,
        measurement_noise_spread, channel_height_kernel.T, sensor_spread_down, sensor_spread_across,
        taper_radius_limit, group_area_number)
    return jnp.transpose(result, (1, 0, 2))[:, :, None, :]


def solution(mesh):
    return jax.shard_map(
        body,
        mesh=mesh,
        in_specs=(P(None, "lev", "region", None), P(None, "lev"), P(), P(), P(), P(), P(), P(), P(), P()),
        out_specs=P(None, "lev", "region", None),
        check_vma=False,
    )
```
